32 devices in a mesh: group: 2 (over y), space: 4 (over z), node: 2 (over core), cuts: 2 (over x).
Axes of the slice: x: 2, y: 2, z: 4, core: 2. Of those that a mesh axis runs over, the one named last changes fastest.
Arguments:
- u_start: float32 [32, 64, 512], P(('group', 'space')), parts along dimension 0, may hold values from -2.5 to 2.5
- kappa: float32 [16, 64, 512], P('space'), may hold values from 0.2 to 2
- source: float32 [2, 32, 64, 512], P('cuts', ('group', 'space')), parts along dimension 1, may hold values from -3 to 3
Outputs:
- solution: float32 [4, 4, 16, 64, 512], P(('group', 'cuts'), 'node', 'space'), parts along dimension 0
The draws below stay inside these ranges and needn't reach their ends.
There are 2 independent parts, one for each index of `group`. The reference program is written for one: setup_inputs(seed, part) draws one part's arguments, and reference() takes and returns one part's arrays. A program takes and returns all parts, laid end to end along the dimension named above; an argument that names none is the same for every part. Nothing has to cross between parts.
All inputs are finite; a program needn't handle non-finite values.
Results may differ from the reference program's by a relative error of at most 0.0003.
Values sent between devices are 32-bit elements; how exact they have to be, the bound alone decides.
A program may use at most 64 MiB of HBM per device.

```python
import math
import jax
import jax.numpy as jnp
import numpy as np
from jax import lax

NX = 64
NY = 512
NODES = 4
SWEEPS = 2
JACOBI = 3
NZ = 16
CUTS = 2


def draw_source(key, part):
    key = jax.random.fold_in(key, 7)
    values = jnp.clip(jax.random.normal(key, (CUTS, NZ, NX, NY), jnp.float32), -3.0, 3.0)
    return values.astype(jnp.float32)


def block_levels(own_key, shape, shards, smallest, top_value):
    def one(dim, shards_of):
        draws = jax.random.uniform(jax.random.fold_in(jax.random.fold_in(own_key, 6), dim), (shards_of,), jnp.float32, smallest / len(shards), top_value / len(shards))
        return jnp.repeat(jnp.exp(draws), shape[dim] // shards_of).reshape((-1,) + (1,) * (len(shape) - dim - 1))

    loudness = one(*shards[0])
    for cut in shards[1:]:
        loudness = loudness * one(*cut)
    return loudness


def normal_values(key, shape, scale, reach, split=(), held_as=jnp.bfloat16):
    values = jax.random.normal(key, shape, jnp.float32) * scale
    if len(split) > 0:
        values = block_levels(key, shape, split, -0.22, 0.18) * values
    return jnp.clip(values, min=-reach, max=reach).astype(held_as)


def setup_inputs(seed: int = 0, part: int = 0) -> dict:
    arg_keys = jax.random.split(jax.random.key(seed), 4)
    part_keys = jax.random.split(jax.random.fold_in(arg_keys[3], part), 4)
    u_start = normal_values(part_keys[0], (NZ, NX, NY), 0.5, 2.5, ((0, 4),), jnp.float32)
    kappa = jnp.clip(jnp.exp(math.log(2.0) - 2.3025851 * jax.random.uniform(arg_keys[1], (NZ, NX, NY), jnp.float32) ** block_levels(arg_keys[1], (NZ, NX, NY), ((0, 4),), -0.2, 0.2)), 0.2, 2.0)
    source = draw_source(jax.random.fold_in(jax.random.fold_in(arg_keys[3], part), 71), part)
    return dict(u_start=u_start, kappa=kappa, source=source)


step_length = 0.5


def radau_tables():
    nodes = [0.08858795951270395, 0.4094668644407347, 0.7876594617608471, 1.0]
    table = []
    for row_node in range(4):
        entries = []
        for basis in range(4):
            coeffs = [1.0]
            for other in range(4):
                if other == basis:
                    continue
                scale = 1.0 / (nodes[basis] - nodes[other])
                longer = [0.0] * (len(coeffs) + 1)
                for power in range(len(coeffs)):
                    longer[power + 1] += coeffs[power] * scale
                    longer[power] -= coeffs[power] * nodes[other] * scale
                coeffs = longer
            integral = 0.0
            for power in range(len(coeffs)):
                integral += coeffs[power] * nodes[row_node] ** (power + 1) / (power + 1)
            entries.append(integral)
        table.append(entries)
    return np.array(table), np.array(nodes) / 4.0


def pad_cells(field):
    return jnp.pad(field, [(0, 0)] * (field.ndim - 3) + [(1, 1)] * 3)


def neighbours(padded):
    return [padded[..., 2:, 1:-1, 1:-1], padded[..., :-2, 1:-1, 1:-1],
            padded[..., 1:-1, 2:, 1:-1], padded[..., 1:-1, :-2, 1:-1],
            padded[..., 1:-1, 1:-1, 2:], padded[..., 1:-1, 1:-1, :-2]]


def couplings(cond_pad):
    centre = cond_pad[..., 1:-1, 1:-1, 1:-1]
    weights = [0.5 * (centre + other) for other in neighbours(cond_pad)]
    diag_sum = weights[0] + weights[1] + weights[2] + weights[3] + weights[4] + weights[5]
    return weights, diag_sum


def flux(weights, field_pad):
    parts = neighbours(field_pad)
    total = weights[0] * parts[0]
    for index in range(1, 6):
        total = total + weights[index] * parts[index]
    return total


def reference(u_start, kappa, source):
    qnp, dnp = radau_tables()
    qmat = jnp.asarray(qnp, jnp.float32)
    delta = jnp.asarray(dnp, jnp.float32)[None, :, None, None, None]
    kappa_pad = pad_cells(kappa)
    state = jnp.broadcast_to(u_start, (CUTS, NODES) + u_start.shape).astype(jnp.float32)
    begin = jnp.broadcast_to(u_start, (CUTS,) + u_start.shape).astype(jnp.float32)
    for sweep in range(SWEEPS):
        if sweep > 0:
            begin = jnp.concatenate([u_start[None], state[:-1, NODES - 1]], 0)
        state_pad = pad_cells(state)
        cond_pad = kappa_pad * (1.0 + state_pad * state_pad)
        weights, diag_sum = couplings(cond_pad)
        operator_state = flux(weights, state_pad) - diag_sum * state
        slope = operator_state + source[:, None]
        combined = jnp.einsum("mj,cjzxy->cmzxy", qmat, slope, precision=lax.Precision.HIGHEST)
        target = begin[:, None] + step_length * combined - step_length * delta * operator_state
        iterate = state
        iterate_pad = state_pad
        for repeat in range(JACOBI):
            if repeat > 0:
                iterate_pad = pad_cells(iterate)
            iterate = (target + step_length * delta * flux(weights, iterate_pad)) / (1.0 + step_length * delta * diag_sum)
        state = iterate
    return state
```

```python
import jax
import jax.numpy as jnp
import numpy as np
from jax import lax
from jax.experimental import pallas as pl
from jax.experimental.pallas import tpu as pltpu
from jax.sharding import PartitionSpec as P

DT = 0.5
MESH = pl.DeviceIdType.MESH
ROWS = 8


def radau_tables():
    nodes = [0.08858795951270396, 0.4094668644407347, 0.7876594617608471, 1.0]
    table = []
    for row_node in range(4):
        entries = []
        for basis in range(4):
            coeffs = [1.0]
            for other in range(4):
                if other == basis:
                    continue
                scale = 1.0 / (nodes[basis] - nodes[other])
                longer = [0.0] * (len(coeffs) + 1)
                for power in range(len(coeffs)):
                    longer[power + 1] += coeffs[power] * scale
                    longer[power] -= coeffs[power] * nodes[other] * scale
                coeffs = longer
            integral = 0.0
            for power in range(len(coeffs)):
                integral += coeffs[power] * nodes[row_node] ** (power + 1) / (power + 1)
            entries.append(integral)
        table.append(entries)
    return (np.array(table), np.array(nodes) / 4.0)


def kernel(peers, slices, u_ref, k_ref, s_ref, out_ref, kap, u0, its, cond, wts, base, oper, dinv, flx, far, beg,
           in_send, in_recv, halo_send, halo_recv, op_send, op_recv, cut_send, cut_recv, fwd_send, fwd_recv):
    depth, nx, ny = u_ref.shape
    top = depth - 1
    qnp, dnp = radau_tables()
    z, nd, cut = lax.axis_index("space"), lax.axis_index("node"), lax.axis_index("cuts")
    has = (z > 0, z < peers - 1)
    next_cut, prev_cut = cut < slices - 1, cut > 0
    last_core = nd == 1

    def pick(low, high):
        return jnp.where(nd == 0, jnp.float32(low), jnp.float32(high))

    step = [pick(DT * dnp[n], DT * dnp[n + 2]) for n in range(2)]
    whole = [pick(DT * qnp[n].sum(), DT * qnp[n + 2].sum()) for n in range(2)]
    own = [[pick(DT * qnp[n, j], DT * qnp[n + 2, j + 2]) for j in range(2)] for n in range(2)]
    away = [[pick(DT * qnp[n, j + 2], DT * qnp[n + 2, j]) for j in range(2)] for n in range(2)]

    row = lax.broadcasted_iota(jnp.int32, (ROWS, ny), 0)
    lane = lax.broadcasted_iota(jnp.int32, (ROWS, ny), 1)
    chunks = nx // ROWS

    def rows(r):
        return slice(r * ROWS, (r + 1) * ROWS)

    def sides(ref, r):
        here = ref(0, r)
        prev = ref(0, r - 1) if r > 0 else here
        succ = ref(0, r + 1) if r < chunks - 1 else here
        return [
            ref(1, r), ref(-1, r),
            pltpu.roll(jnp.where(row == 0, succ, here), ROWS - 1, 0),
            pltpu.roll(jnp.where(row == ROWS - 1, prev, here), 1, 0),
            pltpu.roll(here, ny - 1, 1),
            pltpu.roll(here, 1, 1),
        ]

    def inside(parts, r):
        out = list(parts)
        if r == chunks - 1:
            out[2] = jnp.where(row == ROWS - 1, 0.0, out[2])
        if r == 0:
            out[3] = jnp.where(row == 0, 0.0, out[3])
        out[4] = jnp.where(lane == ny - 1, 0.0, out[4])
        out[5] = jnp.where(lane == 0, 0.0, out[5])
        return out

    def stencil(n, field, p, r):
        half = cond[n, p + 1, rows(r)]
        near = inside(sides(lambda d, q: cond[n, p + 1 + d, rows(q)], r), r)
        w = [half + c for c in near]
        diag = (w[0] + w[1]) + (w[2] + w[3]) + (w[4] + w[5])
        w = inside(w, r)
        v = sides(lambda d, q: field(p + 1 + d, rows(q)), r)
        flow = (w[0] * v[0] + w[1] * v[1]) + (w[2] * v[2] + w[3] * v[3]) + (w[4] * v[4] + w[5] * v[5])
        return w, diag, flow

    def conduct(n, field, index):
        for r in range(chunks):
            v = field(index, rows(r))
            cond[n, index, rows(r)] = 0.5 * kap[index, rows(r)] * (1.0 + v * v)

    def first(p):
        for r in range(chunks):
            w, diag, flow = stencil(0, lambda i, q: u0[i, q], p, r)
            v = u0[p + 1, rows(r)]
            op = flow - diag * v
            slope = op + s_ref[p, rows(r)]
            for n in range(2):
                inv = 1.0 / (1.0 + step[n] * diag)
                t = inv * (v + whole[n] * slope - step[n] * op)
                base[n, p, rows(r)] = t
                scale = step[n] * inv
                for k in range(6):
                    wts[n, k, p, rows(r)] = w[k] * scale
                its[0, n, p + 1, rows(r)] = t + scale * flow

    def second(n, p):
        s = jnp.where(n == 0, step[0], step[1])
        for r in range(chunks):
            w, diag, flow = stencil(n, lambda i, q: its[2, n, i, q], p, r)
            oper[n, p, rows(r)] = flow - diag * its[2, n, p + 1, rows(r)]
            inv = 1.0 / (1.0 + s * diag)
            scale = s * inv
            for k in range(6):
                wts[n, k, p, rows(r)] = w[k] * scale
            dinv[n, p, rows(r)] = inv
            flx[n, p, rows(r)] = scale * flow

    def combine(p):
        for r in range(chunks):
            q = rows(r)
            a, b, c, d = oper[0, p, q], oper[1, p, q], far[0, p, q], far[1, p, q]
            start, src = beg[p, q], s_ref[p, q]
            for n in range(2):
                t = start + own[n][0] * a + own[n][1] * b + away[n][0] * c + away[n][1] * d + whole[n] * src
                t = dinv[n, p, q] * (t - step[n] * (a, b)[n])
                base[n, p, q] = t
                its[3, n, p + 1, q] = t + flx[n, p, q]

    def jacobi(i, n, p):
        for r in range(chunks):
            v = sides(lambda d, q: its[i, n, p + 1 + d, rows(q)], r)
            w = [wts[n, k, p, rows(r)] for k in range(6)]
            got = base[n, p, rows(r)] + (w[0] * v[0] + w[1] * v[1])
            got = got + ((w[2] * v[2] + w[3] * v[3]) + (w[4] * v[4] + w[5] * v[5]))
            if i == 4:
                out_ref[n, p, rows(r)] = got
            else:
                its[i + 1, n, p + 1, rows(r)] = got

    def halo(i, side, n):
        return pltpu.make_async_remote_copy(
            src_ref=its.at[i, n, 1 if side == 0 else depth],
            dst_ref=its.at[i, n, depth + 1 if side == 0 else 0],
            send_sem=halo_send.at[i, side, n], recv_sem=halo_recv.at[i, side, n],
            device_id={"space": z - 1 if side == 0 else z + 1}, device_id_type=MESH)

    def given(side, which):
        src, dst = ((u_ref, u0), (k_ref, kap))[which]
        return pltpu.make_async_remote_copy(
            src_ref=src.at[0 if side == 0 else top],
            dst_ref=dst.at[depth + 1 if side == 0 else 0],
            send_sem=in_send.at[side, which], recv_sem=in_recv.at[side, which],
            device_id={"space": z - 1 if side == 0 else z + 1}, device_id_type=MESH)

    def terms(n, p):
        return pltpu.make_async_remote_copy(
            src_ref=oper.at[n, p], dst_ref=far.at[n, p],
            send_sem=op_send.at[n, p], recv_sem=op_recv.at[n, p],
            device_id={"node": 1 - nd}, device_id_type=MESH)

    def ending(p):
        return pltpu.make_async_remote_copy(
            src_ref=its.at[2, 1, p + 1], dst_ref=beg.at[p],
            send_sem=cut_send.at[p], recv_sem=cut_recv.at[p],
            device_id={"cuts": cut + 1}, device_id_type=MESH)

    def forward(p):
        return pltpu.make_async_remote_copy(
            src_ref=beg.at[p], dst_ref=beg.at[p],
            send_sem=fwd_send.at[p], recv_sem=fwd_recv.at[p],
            device_id={"node": 1 - nd}, device_id_type=MESH)

    barrier = pltpu.get_barrier_semaphore()

    def greet(**where):
        pl.semaphore_signal(barrier, inc=1, device_id=where, device_id_type=MESH)

    @pl.when(has[0])
    def _():
        greet(space=z - 1)

    @pl.when(has[1])
    def _():
        greet(space=z + 1)

    greet(node=1 - nd)

    @pl.when(jnp.logical_and(last_core, next_cut))
    def _():
        greet(cuts=cut + 1)

    @pl.when(jnp.logical_and(last_core, prev_cut))
    def _():
        greet(cuts=cut - 1)

    def one(flag):
        return jnp.where(flag, 1, 0).astype(jnp.int32)

    pl.semaphore_wait(barrier, 1 + one(has[0]) + one(has[1])
                      + one(last_core) * (one(next_cut) + one(prev_cut)))

    for side in range(2):
        @pl.when(has[side])
        def _():
            for which in range(2):
                given(side, which).start()

    for side, index in ((0, 0), (1, depth + 1)):
        @pl.when(jnp.logical_not(has[side]))
        def _():
            zero = jnp.zeros((nx, ny), jnp.float32)
            u0[index] = zero
            kap[index] = zero
            for i in range(5):
                for n in range(2):
                    its[i, n, index] = zero

    def bring(p, carry):
        for r in range(chunks):
            u0[p + 1, rows(r)] = u_ref[p, rows(r)]
            kap[p + 1, rows(r)] = k_ref[p, rows(r)]
        conduct(0, lambda i, q: u0[i, q], p + 1)
        return carry

    def inner(body):
        lax.fori_loop(1, top, lambda p, carry: (body(p), carry)[1], 0)

    lax.fori_loop(0, depth, bring, 0)
    inner(first)
    edges = ((0, 0, 0), (1, top, depth + 1))
    for side, p, index in edges:
        @pl.when(has[side])
        def _():
            for which in range(2):
                given(1 - side, which).wait_recv()
        conduct(0, lambda i, q: u0[i, q], index)
        first(p)

        @pl.when(has[side])
        def _():
            for n in range(2):
                halo(0, side, n).start()

    def sweep_step(i):
        for side, p, index in edges:
            for n in range(2):
                @pl.when(has[side])
                def _():
                    halo(i, 1 - side, n).wait_recv()
                jacobi(i, n, p)
                if i < 4:
                    @pl.when(has[side])
                    def _():
                        halo(i + 1, side, n).start()

        def body(p):
            for n in range(2):
                jacobi(i, n, p)
        inner(body)

    sweep_step(0)
    sweep_step(1)

    @pl.when(jnp.logical_and(last_core, next_cut))
    def _():
        for p in range(depth):
            ending(p).start()

    def both(body):
        lax.fori_loop(0, 2, lambda n, carry: (body(n), carry)[1], 0)

    def state_cond(p):
        for n in range(2):
            conduct(n, lambda i, q: its[2, n, i, q], p + 1)

    lax.fori_loop(0, depth, lambda p, carry: (state_cond(p), carry)[1], 0)

    def middle(p):
        def body(n):
            second(n, p)
            terms(n, p).start()
        both(body)
    inner(middle)
    for side, p, index in edges:
        @pl.when(has[side])
        def _():
            for n in range(2):
                halo(2, 1 - side, n).wait_recv()

        def body(n):
            conduct(n, lambda i, q: its[2, n, i, q], index)
            second(n, p)
            terms(n, p).start()
        both(body)

    @pl.when(jnp.logical_not(prev_cut))
    def _():
        def body(p, carry):
            beg[p] = u_ref[p]
            return carry
        lax.fori_loop(0, depth, body, 0)

    @pl.when(jnp.logical_and(prev_cut, last_core))
    def _():
        for p in range(depth):
            ending(p).wait_recv()
            forward(p).start()

    @pl.when(jnp.logical_and(prev_cut, jnp.logical_not(last_core)))
    def _():
        for p in range(depth):
            forward(p).wait_recv()

    def arrived(p):
        for n in range(2):
            terms(n, p).wait_recv()

    for side, p, index in edges:
        arrived(p)
        combine(p)

        @pl.when(has[side])
        def _():
            for n in range(2):
                halo(3, side, n).start()

    def rest(p):
        arrived(p)
        combine(p)
    inner(rest)
    sweep_step(3)
    sweep_step(4)

    for side in range(2):
        @pl.when(has[side])
        def _():
            for which in range(2):
                given(side, which).wait_send()
            for i in range(5):
                for n in range(2):
                    halo(i, side, n).wait_send()
    for n in range(2):
        for p in range(depth):
            terms(n, p).wait_send()

    @pl.when(jnp.logical_and(last_core, next_cut))
    def _():
        for p in range(depth):
            ending(p).wait_send()

    @pl.when(jnp.logical_and(last_core, prev_cut))
    def _():
        for p in range(depth):
            forward(p).wait_send()


def body(u_start, kappa, source):
    depth, nx, ny = u_start.shape
    f32 = jnp.float32
    peers, slices = lax.axis_size("space"), lax.axis_size("cuts")
    dma = pltpu.SemaphoreType.DMA

    def run(*refs):
        kernel(peers, slices, *refs)

    out = pl.pallas_call(
        run,
        out_shape=jax.ShapeDtypeStruct((2, depth, nx, ny), f32),
        in_specs=[pl.BlockSpec(memory_space=pltpu.VMEM)] * 3,
        out_specs=pl.BlockSpec(memory_space=pltpu.VMEM),
        scratch_shapes=[
            pltpu.VMEM((depth + 2, nx, ny), f32),
            pltpu.VMEM((depth + 2, nx, ny), f32),
            pltpu.VMEM((5, 2, depth + 2, nx, ny), f32),
            pltpu.VMEM((2, depth + 2, nx, ny), f32),
            pltpu.VMEM((2, 6, depth, nx, ny), f32),
            pltpu.VMEM((2, depth, nx, ny), f32),
            pltpu.VMEM((2, depth, nx, ny), f32),
            pltpu.VMEM((2, depth, nx, ny), f32),
            pltpu.VMEM((2, depth, nx, ny), f32),
            pltpu.VMEM((2, depth, nx, ny), f32),
            pltpu.VMEM((depth, nx, ny), f32),
            dma((2, 2)), dma((2, 2)),
            dma((5, 2, 2)), dma((5, 2, 2)),
            dma((2, depth)), dma((2, depth)),
            dma((depth,)), dma((depth,)),
            dma((depth,)), dma((depth,)),
        ],
        compiler_params=pltpu.CompilerParams(
            collective_id=0, has_side_effects=True, vmem_limit_bytes=40 * 1024 * 1024),
    )(u_start, kappa, source[0])
    return out[None]


def solution(mesh):
    placed = (
        P(("group", "space"), None, None),
        P("space", None, None),
        P("cuts", ("group", "space"), None, None),
    )
    return jax.shard_map(
        body,
        mesh=mesh,
        in_specs=placed,
        out_specs=P(("group", "cuts"), "node", "space", None, None),
        check_vma=False,
    )
```

```python
import jax
import jax.numpy as jnp
import numpy as np
from jax import lax
from jax.experimental import pallas as pl
from jax.experimental.pallas import tpu as pltpu
from jax.sharding import PartitionSpec as P

DT = 0.5
MESH = pl.DeviceIdType.MESH
ROWS = 8
WIDE = 4
NEAR = 3


def radau_tables():
    nodes = [0.08858795951270396, 0.4094668644407347, 0.7876594617608471, 1.0]
    table = []
    for row_node in range(4):
        entries = []
        for basis in range(4):
            coeffs = [1.0]
            for other in range(4):
                if other == basis:
                    continue
                scale = 1.0 / (nodes[basis] - nodes[other])
                longer = [0.0] * (len(coeffs) + 1)
                for power in range(len(coeffs)):
                    longer[power + 1] += coeffs[power] * scale
                    longer[power] -= coeffs[power] * nodes[other] * scale
                coeffs = longer
            integral = 0.0
            for power in range(len(coeffs)):
                integral += coeffs[power] * nodes[row_node] ** (power + 1) / (power + 1)
            entries.append(integral)
        table.append(entries)
    return (np.array(table), np.array(nodes) / 4.0)


def kernel(peers, slices, u_ref, k_ref, s_ref, out_ref, kap, u0, srcs, its, cond, wts, base, oper, dinv, flx, far, beg,
           load_sem, in_send, in_recv, pass_send, pass_recv, halo_send, halo_recv, op_send, op_recv, cut_send, cut_recv, fwd_send, fwd_recv):
    depth, nx, ny = u_ref.shape
    top = depth - 1
    qnp, dnp = radau_tables()
    z, nd, cut = lax.axis_index("space"), lax.axis_index("node"), lax.axis_index("cuts")
    has = (z > 0, z < peers - 1)
    next_cut, prev_cut = cut < slices - 1, cut > 0
    last_core = nd == 1

    def pick(low, high):
        return jnp.where(nd == 0, jnp.float32(low), jnp.float32(high))

    step = [pick(DT * dnp[n], DT * dnp[n + 2]) for n in range(2)]
    whole = [pick(DT * qnp[n].sum(), DT * qnp[n + 2].sum()) for n in range(2)]
    own = [[pick(DT * qnp[n, j], DT * qnp[n + 2, j + 2]) for j in range(2)] for n in range(2)]
    away = [[pick(DT * qnp[n, j + 2], DT * qnp[n + 2, j]) for j in range(2)] for n in range(2)]

    row = lax.broadcasted_iota(jnp.int32, (ROWS, ny), 0)
    lane = lax.broadcasted_iota(jnp.int32, (ROWS, ny), 1)
    chunks = nx // ROWS

    def rows(r):
        return slice(r * ROWS, (r + 1) * ROWS)

    def sides(ref, r):
        here = ref(0, r)
        prev = ref(0, r - 1) if r > 0 else here
        succ = ref(0, r + 1) if r < chunks - 1 else here
        return [
            ref(1, r), ref(-1, r),
            pltpu.roll(jnp.where(row == 0, succ, here), ROWS - 1, 0),
            pltpu.roll(jnp.where(row == ROWS - 1, prev, here), 1, 0),
            pltpu.roll(here, ny - 1, 1),
            pltpu.roll(here, 1, 1),
        ]

    def inside(parts, r):
        out = list(parts)
        if r == chunks - 1:
            out[2] = jnp.where(row == ROWS - 1, 0.0, out[2])
        if r == 0:
            out[3] = jnp.where(row == 0, 0.0, out[3])
        out[4] = jnp.where(lane == ny - 1, 0.0, out[4])
        out[5] = jnp.where(lane == 0, 0.0, out[5])
        return out

    def stencil(n, field, p, r):
        half = cond[n, p + WIDE, rows(r)]
        near = inside(sides(lambda d, q: cond[n, p + WIDE + d, rows(q)], r), r)
        w = [half + c for c in near]
        diag = (w[0] + w[1]) + (w[2] + w[3]) + (w[4] + w[5])
        w = inside(w, r)
        v = sides(lambda d, q: field(p + d, rows(q)), r)
        flow = (w[0] * v[0] + w[1] * v[1]) + (w[2] * v[2] + w[3] * v[3]) + (w[4] * v[4] + w[5] * v[5])
        return w, diag, flow

    def start_field(p, q):
        return u0[p + WIDE, q]

    def later_field(n):
        return lambda p, q: its[2, n, p + NEAR, q]

    def conduct(n, field, p):
        for r in range(chunks):
            v = field(p, rows(r))
            cond[n, p + WIDE, rows(r)] = 0.5 * kap[p + WIDE, rows(r)] * (1.0 + v * v)

    def first(p):
        for r in range(chunks):
            w, diag, flow = stencil(0, start_field, p, r)
            v = u0[p + WIDE, rows(r)]
            op = flow - diag * v
            slope = op + srcs[p + WIDE, rows(r)]
            for n in range(2):
                inv = 1.0 / (1.0 + step[n] * diag)
                t = inv * (v + whole[n] * slope - step[n] * op)
                base[n, p + NEAR, rows(r)] = t
                scale = step[n] * inv
                for k in range(6):
                    wts[n, k, p + NEAR, rows(r)] = w[k] * scale
                its[0, n, p + NEAR, rows(r)] = t + scale * flow

    def second(n, p):
        s = jnp.where(n == 0, step[0], step[1])
        for r in range(chunks):
            w, diag, flow = stencil(n, later_field(n), p, r)
            oper[n, p, rows(r)] = flow - diag * its[2, n, p + NEAR, rows(r)]
            inv = 1.0 / (1.0 + s * diag)
            scale = s * inv
            for k in range(6):
                wts[n, k, p + NEAR, rows(r)] = w[k] * scale
            dinv[n, p, rows(r)] = inv
            flx[n, p, rows(r)] = scale * flow

    def combine(p):
        for r in range(chunks):
            q = rows(r)
            a, b, c, d = oper[0, p, q], oper[1, p, q], far[0, p, q], far[1, p, q]
            start, src = beg[p, q], srcs[p + WIDE, q]
            for n in range(2):
                t = start + own[n][0] * a + own[n][1] * b + away[n][0] * c + away[n][1] * d + whole[n] * src
                t = dinv[n, p, q] * (t - step[n] * (a, b)[n])
                base[n, p + NEAR, q] = t
                its[3, n, p + NEAR, q] = t + flx[n, p, q]

    def jacobi(i, n, p):
        for r in range(chunks):
            v = sides(lambda d, q: its[i, n, p + NEAR + d, rows(q)], r)
            w = [wts[n, k, p + NEAR, rows(r)] for k in range(6)]
            got = base[n, p + NEAR, rows(r)] + (w[0] * v[0] + w[1] * v[1])
            got = got + ((w[2] * v[2] + w[3] * v[3]) + (w[4] * v[4] + w[5] * v[5]))
            if i == 4:
                out_ref[n, p, rows(r)] = got
            else:
                its[i + 1, n, p + NEAR, rows(r)] = got

    def halo(i, side, n):
        return pltpu.make_async_remote_copy(
            src_ref=its.at[i, n, NEAR if side == 0 else top + NEAR],
            dst_ref=its.at[i, n, depth + NEAR if side == 0 else NEAR - 1],
            send_sem=halo_send.at[i - 3, side, n], recv_sem=halo_recv.at[i - 3, side, n],
            device_id={"space": z - 1 if side == 0 else z + 1}, device_id_type=MESH)

    given_refs = ((u_ref, u0), (k_ref, kap), (s_ref, srcs))
    items = [(d, which) for d in range(1, WIDE + 1) for which in range(3 if d < WIDE else 2)]
    place = {item: slot for slot, item in enumerate(items)}

    def beyond(side, d):
        return -d if side == 0 else top + d

    def given(side, item):
        d, which = item
        src, dst = given_refs[which]
        return pltpu.make_async_remote_copy(
            src_ref=src.at[d - 1 if side == 0 else depth - d],
            dst_ref=dst.at[beyond(1 - side, d) + WIDE],
            send_sem=in_send.at[side, place[item]], recv_sem=in_recv.at[side, place[item]],
            device_id={"space": z - 1 if side == 0 else z + 1}, device_id_type=MESH)

    def passed(side, item):
        d, which = item
        ref = given_refs[which][1].at[beyond(side, d) + WIDE]
        return pltpu.make_async_remote_copy(
            src_ref=ref, dst_ref=ref,
            send_sem=pass_send.at[side, place[item]], recv_sem=pass_recv.at[side, place[item]],
            device_id={"node": 1 - nd}, device_id_type=MESH)

    def load(which):
        src, dst = given_refs[which]
        return pltpu.make_async_copy(src, dst.at[pl.ds(WIDE, depth)], load_sem.at[which])

    def terms(n, p):
        return pltpu.make_async_remote_copy(
            src_ref=oper.at[n, p], dst_ref=far.at[n, p],
            send_sem=op_send.at[n, p], recv_sem=op_recv.at[n, p],
            device_id={"node": 1 - nd}, device_id_type=MESH)

    def ending(p):
        return pltpu.make_async_remote_copy(
            src_ref=its.at[2, 1, p + NEAR], dst_ref=beg.at[p],
            send_sem=cut_send.at[p], recv_sem=cut_recv.at[p],
            device_id={"cuts": cut + 1}, device_id_type=MESH)

    def forward(p):
        return pltpu.make_async_remote_copy(
            src_ref=beg.at[p], dst_ref=beg.at[p],
            send_sem=fwd_send.at[p], recv_sem=fwd_recv.at[p],
            device_id={"node": 1 - nd}, device_id_type=MESH)

    for which in range(3):
        load(which).start()
    barrier = pltpu.get_barrier_semaphore()

    def greet(**where):
        pl.semaphore_signal(barrier, inc=1, device_id=where, device_id_type=MESH)

    @pl.when(has[0])
    def _():
        greet(space=z - 1)

    @pl.when(has[1])
    def _():
        greet(space=z + 1)

    greet(node=1 - nd)

    @pl.when(jnp.logical_and(last_core, next_cut))
    def _():
        greet(cuts=cut + 1)

    @pl.when(jnp.logical_and(last_core, prev_cut))
    def _():
        greet(cuts=cut - 1)

    def one(flag):
        return jnp.where(flag, 1, 0).astype(jnp.int32)

    pl.semaphore_wait(barrier, 1 + one(has[0]) + one(has[1])
                      + one(last_core) * (one(next_cut) + one(prev_cut)))

    for core in range(2):
        @pl.when(nd == core)
        def _():
            for side in range(2):
                @pl.when(has[side])
                def _():
                    for item in items:
                        if place[item] % 2 == core:
                            given(side, item).start()

    for side in range(2):
        @pl.when(jnp.logical_not(has[side]))
        def _():
            zero = jnp.zeros((nx, ny), jnp.float32)
            p = beyond(side, 1)
            u0[p + WIDE] = zero
            for n in range(2):
                cond[n, p + WIDE] = zero
                for i in range(5):
                    its[i, n, p + NEAR] = zero

    def each(low, high, body):
        lax.fori_loop(low, high, lambda p, carry: (body(p), carry)[1], 0)

    def inner(body):
        each(1, top, body)

    load(0).wait()
    load(1).wait()
    each(0, depth, lambda p: conduct(0, start_field, p))
    load(2).wait()
    inner(first)

    def fetch(d):
        for core in range(2):
            @pl.when(nd == core)
            def _():
                for mine in (True, False):
                    for side in range(2):
                        @pl.when(has[side])
                        def _():
                            for item in items:
                                if item[0] == d and (place[item] % 2 == core) == mine:
                                    if mine:
                                        given(1 - side, item).wait_recv()
                                        passed(side, item).start()
                                    else:
                                        passed(side, item).wait_recv()

    def both_sides(d, body):
        for side in range(2):
            if d > 0:
                @pl.when(has[side])
                def _():
                    body(beyond(side, d))
            else:
                body(beyond(side, d))

    def iterate(i, d):
        def planes(p):
            for n in range(2):
                jacobi(i, n, p)
        if d < 0:
            inner(planes)
        else:
            both_sides(d, planes)

    def stage(d):
        fetch(d)
        both_sides(d, lambda p: conduct(0, start_field, p))
        both_sides(d - 1, first)
        iterate(0, d - 2)
        if d > 1:
            iterate(1, d - 3)

    for d in range(1, WIDE):
        stage(d)

    @pl.when(jnp.logical_and(last_core, next_cut))
    def _():
        for p in range(depth):
            ending(p).start()

    def both(body):
        each(0, 2, body)

    def middle(p):
        def body(n):
            second(n, p)
            terms(n, p).start()
        both(body)

    def state_cond(p):
        for n in range(2):
            conduct(n, later_field(n), p)

    each(0, depth, state_cond)
    inner(middle)
    stage(WIDE)

    edges = ((0, 0), (1, top))
    for side, p in edges:
        @pl.when(has[side])
        def _():
            state_cond(beyond(side, 1))
        middle(p)

    def sweep_step(i):
        for side, p in edges:
            for n in range(2):
                @pl.when(has[side])
                def _():
                    halo(i, 1 - side, n).wait_recv()
                jacobi(i, n, p)
                if i < 4:
                    @pl.when(has[side])
                    def _():
                        halo(i + 1, side, n).start()

        def body(p):
            for n in range(2):
                jacobi(i, n, p)
        inner(body)

    @pl.when(jnp.logical_not(prev_cut))
    def _():
        def body(p, carry):
            beg[p] = u0[p + WIDE]
            return carry
        lax.fori_loop(0, depth, body, 0)

    @pl.when(jnp.logical_and(prev_cut, last_core))
    def _():
        for p in range(depth):
            ending(p).wait_recv()
            forward(p).start()

    @pl.when(jnp.logical_and(prev_cut, jnp.logical_not(last_core)))
    def _():
        for p in range(depth):
            forward(p).wait_recv()

    def arrived(p):
        for n in range(2):
            terms(n, p).wait_recv()

    for side, p in edges:
        arrived(p)
        combine(p)

        @pl.when(has[side])
        def _():
            for n in range(2):
                halo(3, side, n).start()

    def rest(p):
        arrived(p)
        combine(p)
    inner(rest)
    sweep_step(3)
    sweep_step(4)

    for side in range(2):
        @pl.when(has[side])
        def _():
            for i in range(3, 5):
                for n in range(2):
                    halo(i, side, n).wait_send()
    for core in range(2):
        @pl.when(nd == core)
        def _():
            for side in range(2):
                @pl.when(has[side])
                def _():
                    for item in items:
                        if place[item] % 2 == core:
                            given(side, item).wait_send()
                            passed(side, item).wait_send()
    for n in range(2):
        for p in range(depth):
            terms(n, p).wait_send()

    @pl.when(jnp.logical_and(last_core, next_cut))
    def _():
        for p in range(depth):
            ending(p).wait_send()

    @pl.when(jnp.logical_and(last_core, prev_cut))
    def _():
        for p in range(depth):
            forward(p).wait_send()


def body(u_start, kappa, source):
    depth, nx, ny = u_start.shape
    f32 = jnp.float32
    peers, slices = lax.axis_size("space"), lax.axis_size("cuts")
    dma = pltpu.SemaphoreType.DMA

    def run(*refs):
        kernel(peers, slices, *refs)

    out = pl.pallas_call(
        run,
        out_shape=jax.ShapeDtypeStruct((2, depth, nx, ny), f32),
        in_specs=[pl.BlockSpec(memory_space=pltpu.HBM)] * 3,
        out_specs=pl.BlockSpec(memory_space=pltpu.VMEM),
        scratch_shapes=[
            pltpu.VMEM((depth + 2 * WIDE, nx, ny), f32),
            pltpu.VMEM((depth + 2 * WIDE, nx, ny), f32),
            pltpu.VMEM((depth + 2 * WIDE, nx, ny), f32),
            pltpu.VMEM((5, 2, depth + 2 * NEAR, nx, ny), f32),
            pltpu.VMEM((2, depth + 2 * WIDE, nx, ny), f32),
            pltpu.VMEM((2, 6, depth + 2 * NEAR, nx, ny), f32),
            pltpu.VMEM((2, depth + 2 * NEAR, nx, ny), f32),
            pltpu.VMEM((2, depth, nx, ny), f32),
            pltpu.VMEM((2, depth, nx, ny), f32),
            pltpu.VMEM((2, depth, nx, ny), f32),
            pltpu.VMEM((2, depth, nx, ny), f32),
            pltpu.VMEM((depth, nx, ny), f32),
            dma((3,)), dma((2, 11)), dma((2, 11)), dma((2, 11)), dma((2, 11)),
            dma((2, 2, 2)), dma((2, 2, 2)),
            dma((2, depth)), dma((2, depth)),
            dma((depth,)), dma((depth,)),
            dma((depth,)), dma((depth,)),
        ],
        compiler_params=pltpu.CompilerParams(
            collective_id=0, has_side_effects=True, vmem_limit_bytes=52 * 1024 * 1024),
    )(u_start, kappa, source[0])
    return out[None]


def solution(mesh):
    placed = (
        P(("group", "space"), None, None),
        P("space", None, None),
        P("cuts", ("group", "space"), None, None),
    )
    return jax.shard_map(
        body,
        mesh=mesh,
        in_specs=placed,
        out_specs=P(("group", "cuts"), "node", "space", None, None),
        check_vma=False,
    )
```

```python
import jax
import jax.numpy as jnp
import numpy as np
from jax import lax
from jax.experimental import pallas as pl
from jax.experimental.pallas import tpu as pltpu
from jax.sharding import PartitionSpec as P

DT = 0.5
MESH = pl.DeviceIdType.MESH
ROWS = 8
WIDE = 4
NEAR = 3


def radau_tables():
    nodes = [0.08858795951270396, 0.4094668644407347, 0.7876594617608471, 1.0]
    table = []
    for row_node in range(4):
        entries = []
        for basis in range(4):
            coeffs = [1.0]
            for other in range(4):
                if other == basis:
                    continue
                scale = 1.0 / (nodes[basis] - nodes[other])
                longer = [0.0] * (len(coeffs) + 1)
                for power in range(len(coeffs)):
                    longer[power + 1] += coeffs[power] * scale
                    longer[power] -= coeffs[power] * nodes[other] * scale
                coeffs = longer
            integral = 0.0
            for power in range(len(coeffs)):
                integral += coeffs[power] * nodes[row_node] ** (power + 1) / (power + 1)
            entries.append(integral)
        table.append(entries)
    return (np.array(table), np.array(nodes) / 4.0)


def kernel(peers, slices, u_ref, k_ref, s_ref, out_ref, kap, u0, srcs, its, cond, wts, base, oper, dinv, flx, far, beg,
           load_sem, in_send, in_recv, pass_send, pass_recv, halo_send, halo_recv, op_send, op_recv, cut_send, cut_recv, fwd_send, fwd_recv):
    depth, nx, ny = u_ref.shape
    top = depth - 1
    qnp, dnp = radau_tables()
    z, nd, cut = lax.axis_index("space"), lax.axis_index("node"), lax.axis_index("cuts")
    has = (z > 0, z < peers - 1)
    next_cut, prev_cut = cut < slices - 1, cut > 0
    last_core = nd == 1

    def pick(low, high):
        return jnp.where(nd == 0, jnp.float32(low), jnp.float32(high))

    step = [pick(DT * dnp[n], DT * dnp[n + 2]) for n in range(2)]
    whole = [pick(DT * qnp[n].sum(), DT * qnp[n + 2].sum()) for n in range(2)]
    own = [[pick(DT * qnp[n, j], DT * qnp[n + 2, j + 2]) for j in range(2)] for n in range(2)]
    away = [[pick(DT * qnp[n, j + 2], DT * qnp[n + 2, j]) for j in range(2)] for n in range(2)]

    row = lax.broadcasted_iota(jnp.int32, (ROWS, ny), 0)
    lane = lax.broadcasted_iota(jnp.int32, (ROWS, ny), 1)
    chunks = nx // ROWS

    def rows(r):
        return slice(r * ROWS, (r + 1) * ROWS)

    def sides(ref, r):
        here = ref(0, r)
        prev = ref(0, r - 1) if r > 0 else here
        succ = ref(0, r + 1) if r < chunks - 1 else here
        return [
            ref(1, r), ref(-1, r),
            pltpu.roll(jnp.where(row == 0, succ, here), ROWS - 1, 0),
            pltpu.roll(jnp.where(row == ROWS - 1, prev, here), 1, 0),
            pltpu.roll(here, ny - 1, 1),
            pltpu.roll(here, 1, 1),
        ]

    def inside(parts, r):
        out = list(parts)
        if r == chunks - 1:
            out[2] = jnp.where(row == ROWS - 1, 0.0, out[2])
        if r == 0:
            out[3] = jnp.where(row == 0, 0.0, out[3])
        out[4] = jnp.where(lane == ny - 1, 0.0, out[4])
        out[5] = jnp.where(lane == 0, 0.0, out[5])
        return out

    def stencil(n, field, p, r):
        half = cond[n, p + WIDE, rows(r)]
        near = inside(sides(lambda d, q: cond[n, p + WIDE + d, rows(q)], r), r)
        w = [half + c for c in near]
        diag = (w[0] + w[1]) + (w[2] + w[3]) + (w[4] + w[5])
        w = inside(w, r)
        v = sides(lambda d, q: field(p + d, rows(q)), r)
        flow = (w[0] * v[0] + w[1] * v[1]) + (w[2] * v[2] + w[3] * v[3]) + (w[4] * v[4] + w[5] * v[5])
        return w, diag, flow

    def start_field(p, q):
        return u0[p + WIDE, q]

    def later_field(n):
        return lambda p, q: its[2, n, p + NEAR, q]

    def conduct(n, field, p):
        for r in range(chunks):
            v = field(p, rows(r))
            cond[n, p + WIDE, rows(r)] = 0.5 * kap[p + WIDE, rows(r)] * (1.0 + v * v)

    def first(p):
        for r in range(chunks):
            w, diag, flow = stencil(0, start_field, p, r)
            v = u0[p + WIDE, rows(r)]
            op = flow - diag * v
            slope = op + srcs[p + WIDE, rows(r)]
            for n in range(2):
                inv = 1.0 / (1.0 + step[n] * diag)
                t = inv * (v + whole[n] * slope - step[n] * op)
                base[n, p + NEAR, rows(r)] = t
                scale = step[n] * inv
                for k in range(6):
                    wts[n, k, p + NEAR, rows(r)] = w[k] * scale
                its[0, n, p + NEAR, rows(r)] = t + scale * flow

    def second(n, p):
        s = jnp.where(n == 0, step[0], step[1])
        for r in range(chunks):
            w, diag, flow = stencil(n, later_field(n), p, r)
            oper[n, p, rows(r)] = flow - diag * its[2, n, p + NEAR, rows(r)]
            inv = 1.0 / (1.0 + s * diag)
            scale = s * inv
            for k in range(6):
                wts[n, k, p + NEAR, rows(r)] = w[k] * scale
            dinv[n, p, rows(r)] = inv
            flx[n, p, rows(r)] = scale * flow

    def combine(p):
        for r in range(chunks):
            q = rows(r)
            a, b, c, d = oper[0, p, q], oper[1, p, q], far[0, p, q], far[1, p, q]
            start, src = beg[p, q], srcs[p + WIDE, q]
            for n in range(2):
                t = start + own[n][0] * a + own[n][1] * b + away[n][0] * c + away[n][1] * d + whole[n] * src
                t = dinv[n, p, q] * (t - step[n] * (a, b)[n])
                base[n, p + NEAR, q] = t
                its[3, n, p + NEAR, q] = t + flx[n, p, q]

    def jacobi(i, n, p):
        for r in range(chunks):
            v = sides(lambda d, q: its[i, n, p + NEAR + d, rows(q)], r)
            w = [wts[n, k, p + NEAR, rows(r)] for k in range(6)]
            got = base[n, p + NEAR, rows(r)] + (w[0] * v[0] + w[1] * v[1])
            got = got + ((w[2] * v[2] + w[3] * v[3]) + (w[4] * v[4] + w[5] * v[5]))
            if i == 4:
                out_ref[n, p, rows(r)] = got
            else:
                its[i + 1, n, p + NEAR, rows(r)] = got

    def halo(i, side, n):
        return pltpu.make_async_remote_copy(
            src_ref=its.at[i, n, NEAR if side == 0 else top + NEAR],
            dst_ref=its.at[i, n, depth + NEAR if side == 0 else NEAR - 1],
            send_sem=halo_send.at[i - 3, side, n], recv_sem=halo_recv.at[i - 3, side, n],
            device_id={"space": z - 1 if side == 0 else z + 1}, device_id_type=MESH)

    given_refs = ((u_ref, u0), (k_ref, kap), (s_ref, srcs))
    items = [(d, which) for d in range(1, WIDE + 1) for which in range(3 if d < WIDE else 2)]
    place = {item: slot for slot, item in enumerate(items)}

    def beyond(side, d):
        return -d if side == 0 else top + d

    def given(side, item):
        d, which = item
        src, dst = given_refs[which]
        return pltpu.make_async_remote_copy(
            src_ref=src.at[d - 1 if side == 0 else depth - d],
            dst_ref=dst.at[beyond(1 - side, d) + WIDE],
            send_sem=in_send.at[side, place[item]], recv_sem=in_recv.at[side, place[item]],
            device_id={"space": z - 1 if side == 0 else z + 1}, device_id_type=MESH)

    def passed(side, item):
        d, which = item
        ref = given_refs[which][1].at[beyond(side, d) + WIDE]
        return pltpu.make_async_remote_copy(
            src_ref=ref, dst_ref=ref,
            send_sem=pass_send.at[side, place[item]], recv_sem=pass_recv.at[side, place[item]],
            device_id={"node": 1 - nd}, device_id_type=MESH)

    def load(which):
        src, dst = given_refs[which]
        return pltpu.make_async_copy(src, dst.at[pl.ds(WIDE, depth)], load_sem.at[which])

    def terms(n, p):
        return pltpu.make_async_remote_copy(
            src_ref=oper.at[n, p], dst_ref=far.at[n, p],
            send_sem=op_send.at[n, p], recv_sem=op_recv.at[n, p],
            device_id={"node": 1 - nd}, device_id_type=MESH)

    def ending(p):
        return pltpu.make_async_remote_copy(
            src_ref=its.at[2, 1, p + NEAR], dst_ref=beg.at[p],
            send_sem=cut_send.at[p], recv_sem=cut_recv.at[p],
            device_id={"cuts": cut + 1}, device_id_type=MESH)

    def forward(p):
        return pltpu.make_async_remote_copy(
            src_ref=beg.at[p], dst_ref=beg.at[p],
            send_sem=fwd_send.at[p], recv_sem=fwd_recv.at[p],
            device_id={"node": 1 - nd}, device_id_type=MESH)

    for which in range(3):
        load(which).start()
    barrier = pltpu.get_barrier_semaphore()

    def greet(**where):
        pl.semaphore_signal(barrier, inc=1, device_id=where, device_id_type=MESH)

    @pl.when(has[0])
    def _():
        greet(space=z - 1)

    @pl.when(has[1])
    def _():
        greet(space=z + 1)

    greet(node=1 - nd)

    @pl.when(jnp.logical_and(last_core, next_cut))
    def _():
        greet(cuts=cut + 1)

    @pl.when(jnp.logical_and(last_core, prev_cut))
    def _():
        greet(cuts=cut - 1)

    def one(flag):
        return jnp.where(flag, 1, 0).astype(jnp.int32)

    pl.semaphore_wait(barrier, 1 + one(has[0]) + one(has[1])
                      + one(last_core) * (one(next_cut) + one(prev_cut)))

    for core in range(2):
        @pl.when(nd == core)
        def _():
            for side in range(2):
                @pl.when(has[side])
                def _():
                    for item in items:
                        if place[item] % 2 == core:
                            given(side, item).start()

    for side in range(2):
        @pl.when(jnp.logical_not(has[side]))
        def _():
            zero = jnp.zeros((nx, ny), jnp.float32)
            p = beyond(side, 1)
            u0[p + WIDE] = zero
            for n in range(2):
                cond[n, p + WIDE] = zero
                for i in range(5):
                    its[i, n, p + NEAR] = zero

    def each(low, high, body):
        lax.fori_loop(low, high, lambda p, carry: (body(p), carry)[1], 0)

    def inner(body):
        each(1, top, body)

    load(0).wait()
    load(1).wait()
    each(0, depth, lambda p: conduct(0, start_field, p))
    load(2).wait()
    inner(first)

    def fetch(d):
        for core in range(2):
            @pl.when(nd == core)
            def _():
                for mine in (True, False):
                    for side in range(2):
                        @pl.when(has[side])
                        def _():
                            for item in items:
                                if item[0] == d and (place[item] % 2 == core) == mine:
                                    if mine:
                                        given(1 - side, item).wait_recv()
                                        passed(side, item).start()
                                    else:
                                        passed(side, item).wait_recv()

    def both_sides(d, body):
        for side in range(2):
            if d > 0:
                @pl.when(has[side])
                def _():
                    body(beyond(side, d))
            else:
                body(beyond(side, d))

    def iterate(i, d):
        def planes(p):
            for n in range(2):
                jacobi(i, n, p)
        if d < 0:
            inner(planes)
        else:
            both_sides(d, planes)

    def stage(d):
        fetch(d)
        both_sides(d, lambda p: conduct(0, start_field, p))
        both_sides(d - 1, first)
        iterate(0, d - 2)
        if d > 1:
            iterate(1, d - 3)

    within = tuple(range(1, top))

    def hand_over(planes):
        @pl.when(jnp.logical_and(last_core, next_cut))
        def _():
            for p in planes:
                ending(p).start()

    def take_over(planes):
        @pl.when(jnp.logical_and(last_core, prev_cut))
        def _():
            for p in planes:
                ending(p).wait_recv()
                forward(p).start()

    def begun(p):
        @pl.when(jnp.logical_and(prev_cut, jnp.logical_not(last_core)))
        def _():
            forward(p).wait_recv()

    stage(1)
    stage(2)
    hand_over(within)
    stage(3)
    hand_over((0, top))

    def both(body):
        each(0, 2, body)

    def middle(p):
        def body(n):
            second(n, p)
            terms(n, p).start()
        both(body)

    def state_cond(p):
        for n in range(2):
            conduct(n, later_field(n), p)

    each(0, depth, state_cond)
    inner(middle)
    take_over(within)
    stage(WIDE)
    take_over((0, top))

    edges = ((0, 0), (1, top))
    for side, p in edges:
        @pl.when(has[side])
        def _():
            state_cond(beyond(side, 1))
        middle(p)

    def sweep_step(i):
        for n in range(2):
            for side, p in edges:
                @pl.when(has[side])
                def _():
                    halo(i, 1 - side, n).wait_recv()
                jacobi(i, n, p)
                if i < 4:
                    @pl.when(has[side])
                    def _():
                        halo(i + 1, side, n).start()

        def body(p):
            for n in range(2):
                jacobi(i, n, p)
        inner(body)

    @pl.when(jnp.logical_not(prev_cut))
    def _():
        def body(p, carry):
            beg[p] = u0[p + WIDE]
            return carry
        lax.fori_loop(0, depth, body, 0)

    def arrived(p):
        for n in range(2):
            terms(n, p).wait_recv()

    for side, p in edges:
        begun(p)
        arrived(p)
        combine(p)

        @pl.when(has[side])
        def _():
            for n in range(2):
                halo(3, side, n).start()

    def rest(p):
        begun(p)
        arrived(p)
        combine(p)
    inner(rest)
    sweep_step(3)
    sweep_step(4)

    for side in range(2):
        @pl.when(has[side])
        def _():
            for i in range(3, 5):
                for n in range(2):
                    halo(i, side, n).wait_send()
    for core in range(2):
        @pl.when(nd == core)
        def _():
            for side in range(2):
                @pl.when(has[side])
                def _():
                    for item in items:
                        if place[item] % 2 == core:
                            given(side, item).wait_send()
                            passed(side, item).wait_send()
    for n in range(2):
        for p in range(depth):
            terms(n, p).wait_send()

    @pl.when(jnp.logical_and(last_core, next_cut))
    def _():
        for p in range(depth):
            ending(p).wait_send()

    @pl.when(jnp.logical_and(last_core, prev_cut))
    def _():
        for p in range(depth):
            forward(p).wait_send()


def body(u_start, kappa, source):
    depth, nx, ny = u_start.shape
    f32 = jnp.float32
    peers, slices = lax.axis_size("space"), lax.axis_size("cuts")
    dma = pltpu.SemaphoreType.DMA

    def run(*refs):
        kernel(peers, slices, *refs)

    out = pl.pallas_call(
        run,
        out_shape=jax.ShapeDtypeStruct((2, depth, nx, ny), f32),
        in_specs=[pl.BlockSpec(memory_space=pltpu.HBM)] * 3,
        out_specs=pl.BlockSpec(memory_space=pltpu.VMEM),
        scratch_shapes=[
            pltpu.VMEM((depth + 2 * WIDE, nx, ny), f32),
            pltpu.VMEM((depth + 2 * WIDE, nx, ny), f32),
            pltpu.VMEM((depth + 2 * WIDE, nx, ny), f32),
            pltpu.VMEM((5, 2, depth + 2 * NEAR, nx, ny), f32),
            pltpu.VMEM((2, depth + 2 * WIDE, nx, ny), f32),
            pltpu.VMEM((2, 6, depth + 2 * NEAR, nx, ny), f32),
            pltpu.VMEM((2, depth + 2 * NEAR, nx, ny), f32),
            pltpu.VMEM((2, depth, nx, ny), f32),
            pltpu.VMEM((2, depth, nx, ny), f32),
            pltpu.VMEM((2, depth, nx, ny), f32),
            pltpu.VMEM((2, depth, nx, ny), f32),
            pltpu.VMEM((depth, nx, ny), f32),
            dma((3,)), dma((2, 11)), dma((2, 11)), dma((2, 11)), dma((2, 11)),
            dma((2, 2, 2)), dma((2, 2, 2)),
            dma((2, depth)), dma((2, depth)),
            dma((depth,)), dma((depth,)),
            dma((depth,)), dma((depth,)),
        ],
        compiler_params=pltpu.CompilerParams(
            collective_id=0, has_side_effects=True, vmem_limit_bytes=52 * 1024 * 1024),
    )(u_start, kappa, source[0])
    return out[None]


def solution(mesh):
    placed = (
        P(("group", "space"), None, None),
        P("space", None, None),
        P("cuts", ("group", "space"), None, None),
    )
    return jax.shard_map(
        body,
        mesh=mesh,
        in_specs=placed,
        out_specs=P(("group", "cuts"), "node", "space", None, None),
        check_vma=False,
    )
```

```python
import jax
import jax.numpy as jnp
import numpy as np
from jax import lax
from jax.experimental import pallas as pl
from jax.experimental.pallas import tpu as pltpu
from jax.sharding import PartitionSpec as P

DT = 0.5
MESH = pl.DeviceIdType.MESH
ROWS = 8


def radau_tables():
    nodes = [0.08858795951270396, 0.4094668644407347, 0.7876594617608471, 1.0]
    table = []
    for row_node in range(4):
        entries = []
        for basis in range(4):
            coeffs = [1.0]
            for other in range(4):
                if other == basis:
                    continue
                scale = 1.0 / (nodes[basis] - nodes[other])
                longer = [0.0] * (len(coeffs) + 1)
                for power in range(len(coeffs)):
                    longer[power + 1] += coeffs[power] * scale
                    longer[power] -= coeffs[power] * nodes[other] * scale
                coeffs = longer
            integral = 0.0
            for power in range(len(coeffs)):
                integral += coeffs[power] * nodes[row_node] ** (power + 1) / (power + 1)
            entries.append(integral)
        table.append(entries)
    return (np.array(table), np.array(nodes) / 4.0)


def kernel(peers, slices, u_ref, k_ref, s_ref, out_ref, kap, u0, its, cond, wts, base, oper, dinv, flx, far, beg,
           in_send, in_recv, halo_send, halo_recv, op_send, op_recv, cut_send, cut_recv, fwd_send, fwd_recv):
    depth, nx, ny = u_ref.shape
    top = depth - 1
    qnp, dnp = radau_tables()
    z, nd, cut = lax.axis_index("space"), lax.axis_index("node"), lax.axis_index("cuts")
    has = (z > 0, z < peers - 1)
    next_cut, prev_cut = cut < slices - 1, cut > 0
    last_core = nd == 1

    def pick(low, high):
        return jnp.where(nd == 0, jnp.float32(low), jnp.float32(high))

    step = [pick(DT * dnp[n], DT * dnp[n + 2]) for n in range(2)]
    whole = [pick(DT * qnp[n].sum(), DT * qnp[n + 2].sum()) for n in range(2)]
    own = [[pick(DT * qnp[n, j], DT * qnp[n + 2, j + 2]) for j in range(2)] for n in range(2)]
    away = [[pick(DT * qnp[n, j + 2], DT * qnp[n + 2, j]) for j in range(2)] for n in range(2)]

    row = lax.broadcasted_iota(jnp.int32, (ROWS, ny), 0)
    lane = lax.broadcasted_iota(jnp.int32, (ROWS, ny), 1)
    chunks = nx // ROWS

    def rows(r):
        return slice(r * ROWS, (r + 1) * ROWS)

    def sides(ref, r):
        here = ref(0, r)
        prev = ref(0, r - 1) if r > 0 else here
        succ = ref(0, r + 1) if r < chunks - 1 else here
        return [
            ref(1, r), ref(-1, r),
            pltpu.roll(jnp.where(row == 0, succ, here), ROWS - 1, 0),
            pltpu.roll(jnp.where(row == ROWS - 1, prev, here), 1, 0),
            pltpu.roll(here, ny - 1, 1),
            pltpu.roll(here, 1, 1),
        ]

    def inside(parts, r):
        out = list(parts)
        if r == chunks - 1:
            out[2] = jnp.where(row == ROWS - 1, 0.0, out[2])
        if r == 0:
            out[3] = jnp.where(row == 0, 0.0, out[3])
        out[4] = jnp.where(lane == ny - 1, 0.0, out[4])
        out[5] = jnp.where(lane == 0, 0.0, out[5])
        return out

    def stencil(n, field, p, r):
        half = cond[n, p + 1, rows(r)]
        near = inside(sides(lambda d, q: cond[n, p + 1 + d, rows(q)], r), r)
        w = [half + c for c in near]
        diag = (w[0] + w[1]) + (w[2] + w[3]) + (w[4] + w[5])
        w = inside(w, r)
        v = sides(lambda d, q: field(p + 1 + d, rows(q)), r)
        flow = (w[0] * v[0] + w[1] * v[1]) + (w[2] * v[2] + w[3] * v[3]) + (w[4] * v[4] + w[5] * v[5])
        return w, diag, flow

    def conduct(n, field, index):
        for r in range(chunks):
            v = field(index, rows(r))
            cond[n, index, rows(r)] = 0.5 * kap[index, rows(r)] * (1.0 + v * v)

    def first(p):
        for r in range(chunks):
            w, diag, flow = stencil(0, lambda i, q: u0[i, q], p, r)
            v = u0[p + 1, rows(r)]
            op = flow - diag * v
            slope = op + s_ref[p, rows(r)]
            for n in range(2):
                inv = 1.0 / (1.0 + step[n] * diag)
                t = inv * (v + whole[n] * slope - step[n] * op)
                base[n, p, rows(r)] = t
                scale = step[n] * inv
                for k in range(6):
                    wts[n, k, p, rows(r)] = w[k] * scale
                its[0, n, p + 1, rows(r)] = t + scale * flow

    def second(n, p):
        s = jnp.where(n == 0, step[0], step[1])
        for r in range(chunks):
            w, diag, flow = stencil(n, lambda i, q: its[2, n, i, q], p, r)
            oper[n, p, rows(r)] = flow - diag * its[2, n, p + 1, rows(r)]
            inv = 1.0 / (1.0 + s * diag)
            scale = s * inv
            for k in range(6):
                wts[n, k, p, rows(r)] = w[k] * scale
            dinv[n, p, rows(r)] = inv
            flx[n, p, rows(r)] = scale * flow

    def combine(p):
        for r in range(chunks):
            q = rows(r)
            a, b, c, d = oper[0, p, q], oper[1, p, q], far[0, p, q], far[1, p, q]
            start, src = beg[p, q], s_ref[p, q]
            for n in range(2):
                t = start + own[n][0] * a + own[n][1] * b + away[n][0] * c + away[n][1] * d + whole[n] * src
                t = dinv[n, p, q] * (t - step[n] * (a, b)[n])
                base[n, p, q] = t
                its[3, n, p + 1, q] = t + flx[n, p, q]

    def jacobi(i, n, p):
        for r in range(chunks):
            v = sides(lambda d, q: its[i, n, p + 1 + d, rows(q)], r)
            w = [wts[n, k, p, rows(r)] for k in range(6)]
            got = base[n, p, rows(r)] + (w[0] * v[0] + w[1] * v[1])
            got = got + ((w[2] * v[2] + w[3] * v[3]) + (w[4] * v[4] + w[5] * v[5]))
            if i == 4:
                out_ref[n, p, rows(r)] = got
            else:
                its[i + 1, n, p + 1, rows(r)] = got

    def halo(i, side, n):
        return pltpu.make_async_remote_copy(
            src_ref=its.at[i, n, 1 if side == 0 else depth],
            dst_ref=its.at[i, n, depth + 1 if side == 0 else 0],
            send_sem=halo_send.at[i, side, n], recv_sem=halo_recv.at[i, side, n],
            device_id={"space": z - 1 if side == 0 else z + 1}, device_id_type=MESH)

    def given(side, which):
        src, dst = ((u_ref, u0), (k_ref, kap))[which]
        return pltpu.make_async_remote_copy(
            src_ref=src.at[0 if side == 0 else top],
            dst_ref=dst.at[depth + 1 if side == 0 else 0],
            send_sem=in_send.at[side, which], recv_sem=in_recv.at[side, which],
            device_id={"space": z - 1 if side == 0 else z + 1}, device_id_type=MESH)

    def terms(n, p):
        return pltpu.make_async_remote_copy(
            src_ref=oper.at[n, p], dst_ref=far.at[n, p],
            send_sem=op_send.at[n, p], recv_sem=op_recv.at[n, p],
            device_id={"node": 1 - nd}, device_id_type=MESH)

    def ending(p):
        return pltpu.make_async_remote_copy(
            src_ref=its.at[2, 1, p + 1], dst_ref=beg.at[p],
            send_sem=cut_send.at[p], recv_sem=cut_recv.at[p],
            device_id={"cuts": cut + 1}, device_id_type=MESH)

    def forward(p):
        return pltpu.make_async_remote_copy(
            src_ref=beg.at[p], dst_ref=beg.at[p],
            send_sem=fwd_send.at[p], recv_sem=fwd_recv.at[p],
            device_id={"node": 1 - nd}, device_id_type=MESH)

    barrier = pltpu.get_barrier_semaphore()

    def greet(**where):
        pl.semaphore_signal(barrier, inc=1, device_id=where, device_id_type=MESH)

    @pl.when(has[0])
    def _():
        greet(space=z - 1)

    @pl.when(has[1])
    def _():
        greet(space=z + 1)

    greet(node=1 - nd)

    @pl.when(jnp.logical_and(last_core, next_cut))
    def _():
        greet(cuts=cut + 1)

    @pl.when(jnp.logical_and(last_core, prev_cut))
    def _():
        greet(cuts=cut - 1)

    def one(flag):
        return jnp.where(flag, 1, 0).astype(jnp.int32)

    pl.semaphore_wait(barrier, 1 + one(has[0]) + one(has[1])
                      + one(last_core) * (one(next_cut) + one(prev_cut)))

    for side in range(2):
        @pl.when(has[side])
        def _():
            for which in range(2):
                given(side, which).start()

    for side, index in ((0, 0), (1, depth + 1)):
        @pl.when(jnp.logical_not(has[side]))
        def _():
            zero = jnp.zeros((nx, ny), jnp.float32)
            u0[index] = zero
            kap[index] = zero
            for i in range(5):
                for n in range(2):
                    its[i, n, index] = zero

    def bring(p, carry):
        for r in range(chunks):
            u0[p + 1, rows(r)] = u_ref[p, rows(r)]
            kap[p + 1, rows(r)] = k_ref[p, rows(r)]
        conduct(0, lambda i, q: u0[i, q], p + 1)
        return carry

    def inner(body):
        lax.fori_loop(1, top, lambda p, carry: (body(p), carry)[1], 0)

    lax.fori_loop(0, depth, bring, 0)
    inner(first)
    edges = ((0, 0, 0), (1, top, depth + 1))
    for side, p, index in edges:
        @pl.when(has[side])
        def _():
            for which in range(2):
                given(1 - side, which).wait_recv()
        conduct(0, lambda i, q: u0[i, q], index)
        first(p)

        @pl.when(has[side])
        def _():
            for n in range(2):
                halo(0, side, n).start()

    def sweep_step(i):
        for n in range(2):
            for side, p, index in edges:
                @pl.when(has[side])
                def _():
                    halo(i, 1 - side, n).wait_recv()
                jacobi(i, n, p)
                if i < 4:
                    @pl.when(has[side])
                    def _():
                        halo(i + 1, side, n).start()

        def body(p):
            for n in range(2):
                jacobi(i, n, p)
        inner(body)

    sweep_step(0)
    sweep_step(1)

    @pl.when(jnp.logical_and(last_core, next_cut))
    def _():
        for p in range(depth):
            ending(p).start()

    def both(body):
        lax.fori_loop(0, 2, lambda n, carry: (body(n), carry)[1], 0)

    def state_cond(p):
        for n in range(2):
            conduct(n, lambda i, q: its[2, n, i, q], p + 1)

    lax.fori_loop(0, depth, lambda p, carry: (state_cond(p), carry)[1], 0)

    def middle(p):
        def body(n):
            second(n, p)
            terms(n, p).start()
        both(body)
    inner(middle)
    for side, p, index in edges:
        @pl.when(has[side])
        def _():
            for n in range(2):
                halo(2, 1 - side, n).wait_recv()

        def body(n):
            conduct(n, lambda i, q: its[2, n, i, q], index)
            second(n, p)
            terms(n, p).start()
        both(body)

    @pl.when(jnp.logical_not(prev_cut))
    def _():
        def body(p, carry):
            beg[p] = u_ref[p]
            return carry
        lax.fori_loop(0, depth, body, 0)

    @pl.when(jnp.logical_and(prev_cut, last_core))
    def _():
        for p in range(depth):
            ending(p).wait_recv()
            forward(p).start()

    @pl.when(jnp.logical_and(prev_cut, jnp.logical_not(last_core)))
    def _():
        for p in range(depth):
            forward(p).wait_recv()

    def arrived(p):
        for n in range(2):
            terms(n, p).wait_recv()

    for side, p, index in edges:
        arrived(p)
        combine(p)

        @pl.when(has[side])
        def _():
            for n in range(2):
                halo(3, side, n).start()

    def rest(p):
        arrived(p)
        combine(p)
    inner(rest)
    sweep_step(3)
    sweep_step(4)

    for side in range(2):
        @pl.when(has[side])
        def _():
            for which in range(2):
                given(side, which).wait_send()
            for i in range(5):
                for n in range(2):
                    halo(i, side, n).wait_send()
    for n in range(2):
        for p in range(depth):
            terms(n, p).wait_send()

    @pl.when(jnp.logical_and(last_core, next_cut))
    def _():
        for p in range(depth):
            ending(p).wait_send()

    @pl.when(jnp.logical_and(last_core, prev_cut))
    def _():
        for p in range(depth):
            forward(p).wait_send()


def body(u_start, kappa, source):
    depth, nx, ny = u_start.shape
    f32 = jnp.float32
    peers, slices = lax.axis_size("space"), lax.axis_size("cuts")
    dma = pltpu.SemaphoreType.DMA

    def run(*refs):
        kernel(peers, slices, *refs)

    out = pl.pallas_call(
        run,
        out_shape=jax.ShapeDtypeStruct((2, depth, nx, ny), f32),
        in_specs=[pl.BlockSpec(memory_space=pltpu.VMEM)] * 3,
        out_specs=pl.BlockSpec(memory_space=pltpu.VMEM),
        scratch_shapes=[
            pltpu.VMEM((depth + 2, nx, ny), f32),
            pltpu.VMEM((depth + 2, nx, ny), f32),
            pltpu.VMEM((5, 2, depth + 2, nx, ny), f32),
            pltpu.VMEM((2, depth + 2, nx, ny), f32),
            pltpu.VMEM((2, 6, depth, nx, ny), f32),
            pltpu.VMEM((2, depth, nx, ny), f32),
            pltpu.VMEM((2, depth, nx, ny), f32),
            pltpu.VMEM((2, depth, nx, ny), f32),
            pltpu.VMEM((2, depth, nx, ny), f32),
            pltpu.VMEM((2, depth, nx, ny), f32),
            pltpu.VMEM((depth, nx, ny), f32),
            dma((2, 2)), dma((2, 2)),
            dma((5, 2, 2)), dma((5, 2, 2)),
            dma((2, depth)), dma((2, depth)),
            dma((depth,)), dma((depth,)),
            dma((depth,)), dma((depth,)),
        ],
        compiler_params=pltpu.CompilerParams(
            collective_id=0, has_side_effects=True, vmem_limit_bytes=40 * 1024 * 1024),
    )(u_start, kappa, source[0])
    return out[None]


def solution(mesh):
    placed = (
        P(("group", "space"), None, None),
        P("space", None, None),
        P("cuts", ("group", "space"), None, None),
    )
    return jax.shard_map(
        body,
        mesh=mesh,
        in_specs=placed,
        out_specs=P(("group", "cuts"), "node", "space", None, None),
        check_vma=False,
    )
```
